32 devices in a mesh: row: 4 (over z), col: 4 (over y, x), rep: 2 (over core).
Axes of the slice: x: 2, y: 2, z: 4, core: 2. Of those that a mesh axis runs over, the one named last changes fastest.
Arguments:
- pair: bfloat16 [512, 512, 128], P('row', 'col'), may hold values from -8 to 8
- w_left: bfloat16 [2, 128, 128], P(None, None, 'rep'), may hold values from -1 to 1
- w_left_gate: bfloat16 [2, 128, 128], P(None, None, 'rep'), may hold values from -0.5 to 0.5
- w_right: bfloat16 [2, 128, 128], P(None, None, 'rep'), may hold values from -0.5 to 0.5
- w_right_gate: bfloat16 [2, 128, 128], P(None, None, 'rep'), may hold values from -0.5 to 0.5
- w_gate: bfloat16 [2, 128, 128], replicated, may hold values from -0.5 to 0.5
- w_out: bfloat16 [2, 128, 128], P(None, 'rep'), may hold values from -0.5 to 0.5
- w_trans_in: bfloat16 [128, 1024], replicated, may hold values from -0.5 to 0.5
- w_trans_out: bfloat16 [512, 128], replicated, may hold values from -0.25 to 0.25
Outputs:
- updated: bfloat16 [512, 512, 128], P('row', ('col', 'rep'))
The draws below stay inside these ranges and needn't reach their ends.
All inputs are finite; a program needn't handle non-finite values.
Results may differ from the reference program's by a relative error of at most 0.013.
Values may be sent and summed in bfloat16 or wider, within the bound.
A program may use at most 192 MiB of HBM per device.

```python
import math
import jax
import jax.numpy as jnp
from jax import lax

C = 128
CH = 128
TR = 512
NPAIR = 512


def draw_pair(key, part):
    key = jax.random.fold_in(key, 1)
    keys = jax.random.split(key, 4)
    base = jax.random.normal(keys[0], (NPAIR, NPAIR, C), jnp.float32)
    row_scale = jnp.exp(jax.random.uniform(keys[1], (NPAIR, 1, 1), jnp.float32, -1.15, 1.15))
    col_scale = jnp.exp(jax.random.uniform(keys[2], (1, NPAIR, 1), jnp.float32, -0.5, 0.5))
    chan_scale = jnp.exp(jax.random.uniform(keys[3], (1, 1, C), jnp.float32, -1.15, 1.15))
    return jnp.clip(base * row_scale * col_scale * chan_scale, -8.0, 8.0).astype(jnp.bfloat16)


def draw_w_left(key, part):
    key = jax.random.fold_in(key, 2)
    keys = jax.random.split(key, 2)
    base = jax.random.normal(keys[0], (2, C, CH), jnp.float32)
    rising = jnp.exp(math.log(3.0) * (jnp.arange(CH, dtype=jnp.float32) / CH - 0.5))
    spread = jnp.exp(jax.random.uniform(keys[1], (2, 1, CH), jnp.float32, -0.7, 0.7))
    return jnp.clip(base * C ** (-0.5) * rising * spread, -1.0, 1.0).astype(jnp.bfloat16)


def block_levels(own_key, dims, cuts, least, largest):
    level, own = 1.0, jax.random.fold_in(own_key, 6)
    for position, blocks in cuts:
        heights = jnp.exp(jax.random.uniform(jax.random.fold_in(own, position), (blocks,), jnp.float32, least / len(cuts), largest / len(cuts)))
        level = level * jnp.repeat(heights, dims[position] // blocks).reshape([-1 if axis == position else 1 for axis in range(len(dims))])
    return level


def centred(rng, extent, deviation, reach, pieces=(), kind=jnp.bfloat16):
    drawn = jax.random.normal(rng, extent, jnp.float32) * deviation
    if len(pieces) > 0:
        drawn = block_levels(rng, extent, pieces, -0.22, 0.18) * drawn
    return jnp.clip(drawn, min=-reach, max=reach).astype(kind)


def setup_inputs(seed: int = 0) -> dict:
    arg_keys = jax.random.split(jax.random.key(seed), 10)
    pair = draw_pair(jax.random.fold_in(arg_keys[9], 71), 0)
    w_left = draw_w_left(jax.random.fold_in(arg_keys[9], 71), 0)
    w_left_gate = centred(arg_keys[2], (2, C, CH), C ** -0.5, 0.5, ((2, 2),))
    w_right = centred(arg_keys[3], (2, C, CH), C ** -0.5, 0.5, ((2, 2),))
    w_right_gate = centred(arg_keys[4], (2, C, CH), C ** -0.5, 0.5, ((2, 2),))
    w_gate = centred(arg_keys[5], (2, C, C), C ** -0.5, 0.5)
    w_out = centred(arg_keys[6], (2, CH, C), CH ** -0.5, 0.5, ((1, 2),))
    w_trans_in = centred(arg_keys[7], (C, 2 * TR), C ** -0.5, 0.5)
    w_trans_out = centred(arg_keys[8], (TR, C), TR ** -0.5, 0.25)
    return dict(pair=pair, w_left=w_left, w_left_gate=w_left_gate, w_right=w_right, w_right_gate=w_right_gate, w_gate=w_gate, w_out=w_out, w_trans_in=w_trans_in, w_trans_out=w_trans_out)


epsilon = 1e-05

def normalize(values, axis):
    mean_value = lax.optimization_barrier(jnp.mean(values, axis, keepdims=True))
    square_mean = lax.optimization_barrier(jnp.mean(values * values, axis, keepdims=True))
    return (values - mean_value) * lax.rsqrt(square_mean - mean_value * mean_value + epsilon)

def run_blocks(func, total, size):
    starts = jnp.arange(total // size, dtype=jnp.int32) * size
    return lax.map(func, starts)

def update(state, left_w, left_g, right_w, right_g, gate_w, out_w, outgoing):
    npair = state.shape[0]
    size = math.gcd(npair, 64)
    f32 = jnp.float32

    def project(first_row):
        rows = lax.dynamic_slice_in_dim(state, first_row, size, 0)
        normed = normalize(rows, 2).astype(jnp.bfloat16).astype(f32)

        def linear(weight):
            return jnp.einsum('ikd,dc->cik', normed, weight.astype(f32), precision=lax.Precision.HIGHEST)
        left_vals = (jax.nn.sigmoid(linear(left_g)) * linear(left_w)).astype(jnp.bfloat16)
        right_vals = (jax.nn.sigmoid(linear(right_g)) * linear(right_w)).astype(jnp.bfloat16)
        return (left_vals, right_vals)
    lefts, rights = run_blocks(project, npair, size)
    channels = lefts.shape[1]
    left_all = jnp.transpose(lefts, (1, 0, 2, 3)).reshape(channels, npair, npair)
    right_all = jnp.transpose(rights, (1, 0, 2, 3)).reshape(channels, npair, npair)

    def channel_product(operands):
        left_mat = operands[0].astype(f32)
        right_mat = operands[1].astype(f32)
        if outgoing:
            return jnp.dot(left_mat, right_mat.T, precision=lax.Precision.HIGHEST)
        return jnp.dot(left_mat.T, right_mat, precision=lax.Precision.HIGHEST)
    hidden = lax.map(channel_product, (left_all, right_all))

    def finish(first_row):
        rows = lax.dynamic_slice_in_dim(state, first_row, size, 0)
        normed = normalize(rows, 2).astype(jnp.bfloat16).astype(f32)
        gate_values = jax.nn.sigmoid(jnp.einsum('ikd,de->ike', normed, gate_w.astype(f32), precision=lax.Precision.HIGHEST))
        block_hidden = lax.dynamic_slice_in_dim(hidden, first_row, size, 1)
        scaled = normalize(block_hidden, 0).astype(jnp.bfloat16).astype(f32)
        projected = jnp.einsum('cik,cd->ikd', scaled, out_w.astype(f32), precision=lax.Precision.HIGHEST)
        return rows + gate_values * projected
    return run_blocks(finish, npair, size).reshape(state.shape)

def transition(state, w_trans_in, w_trans_out):
    npair = state.shape[0]
    size = math.gcd(npair, 64)
    f32 = jnp.float32
    width = w_trans_out.shape[0]

    def block_fn(first_row):
        rows = lax.dynamic_slice_in_dim(state, first_row, size, 0)
        normed = normalize(rows, 2).astype(jnp.bfloat16).astype(f32)
        inner = jnp.einsum('ijd,de->ije', normed, w_trans_in.astype(f32), precision=lax.Precision.HIGHEST)
        active = (jax.nn.silu(inner[..., :width]) * inner[..., width:]).astype(jnp.bfloat16).astype(f32)
        return (rows + jnp.einsum('ije,ed->ijd', active, w_trans_out.astype(f32), precision=lax.Precision.HIGHEST)).astype(jnp.bfloat16)
    return run_blocks(block_fn, npair, size).reshape(state.shape)

def reference(pair, w_left, w_left_gate, w_right, w_right_gate, w_gate, w_out, w_trans_in, w_trans_out):
    state = pair.astype(jnp.float32)
    state = update(state, w_left[0], w_left_gate[0], w_right[0], w_right_gate[0], w_gate[0], w_out[0], True)
    state = update(state, w_left[1], w_left_gate[1], w_right[1], w_right_gate[1], w_gate[1], w_out[1], False)
    return transition(state, w_trans_in, w_trans_out)
```

```python
import jax
import jax.numpy as jnp
from jax import lax
from jax.sharding import PartitionSpec as P

epsilon = 1e-05
ALL = ("row", "col", "rep")


def normalize(values, axis):
    mean_value = jnp.mean(values, axis, keepdims=True)
    square_mean = jnp.mean(values * values, axis, keepdims=True)
    return (values - mean_value) * lax.rsqrt(square_mean - mean_value * mean_value + epsilon)


def exchange(values, axes):
    return lax.all_to_all(values, axes, split_axis=0, concat_axis=0, tiled=True)


def gated(normed, w_value, w_gate):
    value = jnp.einsum("abd,dc->cab", normed, w_value, preferred_element_type=jnp.float32)
    gate = jnp.einsum("abd,dc->cab", normed, w_gate, preferred_element_type=jnp.float32)
    return (jax.nn.sigmoid(gate) * value).astype(jnp.bfloat16)


def finish(state, normed, returned, w_gate, w_out):
    scaled = normalize(returned.astype(jnp.float32), 0).astype(jnp.bfloat16)
    projected = jnp.einsum("cji,cd->jid", scaled, w_out, preferred_element_type=jnp.float32)
    gate = jax.nn.sigmoid(
        jnp.einsum("jid,de->jie", normed, w_gate, preferred_element_type=jnp.float32)
    )
    return state + gate * projected


def send_back(right_all, left_all):
    rows, cols, reps = (lax.axis_size(name) for name in ALL)
    per_device, npair, _ = right_all.shape
    products = jnp.einsum(
        "cjk,cik->cji", right_all, left_all, preferred_element_type=jnp.float32
    ).astype(jnp.bfloat16)
    width = npair // (cols * reps)
    height = npair // rows
    grid = products.reshape(per_device, cols, reps, width, rows, height)
    outbound = jnp.transpose(grid, (4, 1, 2, 0, 3, 5)).reshape(-1, per_device, width, height)
    return exchange(outbound, ALL).reshape(-1, width, height)


def on_device(
    pair, w_left, w_left_gate, w_right, w_right_gate, w_gate, w_out, w_trans_in, w_trans_out
):
    rows, cols, reps = (lax.axis_size(name) for name in ALL)
    height, full_width, _ = pair.shape
    width = full_width // reps
    channels = w_left.shape[2] * reps
    per_device = channels // (rows * cols * reps)
    out_all = lax.all_gather(w_out, "rep", axis=1)
    out_all = jnp.transpose(
        out_all.reshape(2, reps, rows * cols, per_device, -1), (0, 2, 1, 3, 4)
    ).reshape(2, channels, -1)
    side = jnp.stack([w_left[1], w_left_gate[1], w_right[1], w_right_gate[1]])
    side = lax.all_gather(side, "rep", axis=2)
    side = jnp.transpose(
        side.reshape(4, -1, reps, rows * cols, per_device), (0, 1, 3, 2, 4)
    ).reshape(4, -1, channels)

    normed = normalize(pair.astype(jnp.float32), 2).astype(jnp.bfloat16)

    def spread0(value, gate):
        tile = gated(normed, value, gate)
        got = exchange(tile.reshape(rows * cols, per_device, height, full_width), ("row", "col"))
        grid = got.reshape(rows, cols, per_device, height, full_width)
        return jnp.transpose(grid, (2, 0, 3, 1, 4)).reshape(
            per_device, rows * height, cols * full_width
        )

    left_all = spread0(w_left[0], w_left_gate[0])
    right_all = spread0(w_right[0], w_right_gate[0])
    returned = send_back(right_all, left_all)
    half = lax.dynamic_slice_in_dim(pair, lax.axis_index("rep") * width, width, 1)
    state = jnp.transpose(half, (1, 0, 2)).astype(jnp.float32)
    normed_half = normalize(state, 2).astype(jnp.bfloat16)
    state = finish(state, normed_half, returned, w_gate[0], out_all[0])

    normed = normalize(state, 2).astype(jnp.bfloat16)

    def spread1(value, gate):
        tile = gated(normed, value, gate)
        got = exchange(tile.reshape(rows * cols * reps, per_device, width, height), ALL)
        grid = got.reshape(rows, cols * reps, per_device, width, height)
        return jnp.transpose(grid, (2, 1, 3, 0, 4)).reshape(
            per_device, cols * full_width, rows * height
        )

    left_all = spread1(side[0], side[1])
    right_all = spread1(side[2], side[3])
    returned = send_back(right_all, left_all)
    state = finish(state, normed, returned, w_gate[1], out_all[1])

    normed = normalize(state, 2).astype(jnp.bfloat16)
    hidden = w_trans_out.shape[0]
    inner = jnp.einsum("jid,de->jie", normed, w_trans_in, preferred_element_type=jnp.float32)
    active = (jax.nn.silu(inner[..., :hidden]) * inner[..., hidden:]).astype(jnp.bfloat16)
    updated = state + jnp.einsum(
        "jie,ed->jid", active, w_trans_out, preferred_element_type=jnp.float32
    )
    return jnp.transpose(updated.astype(jnp.bfloat16), (1, 0, 2))


def solution(mesh):
    placed = (
        P("row", "col", None),
        P(None, None, "rep"),
        P(None, None, "rep"),
        P(None, None, "rep"),
        P(None, None, "rep"),
        P(),
        P(None, "rep", None),
        P(),
        P(),
    )
    return jax.shard_map(
        on_device,
        mesh=mesh,
        in_specs=placed,
        out_specs=P("row", ("col", "rep"), None),
        check_vma=False,
    )
```

```python
import functools

import jax
import jax.numpy as jnp
from jax import lax
from jax.experimental import pallas as pl
from jax.experimental.pallas import tpu as pltpu
from jax.sharding import PartitionSpec as P

epsilon = 1e-05
ALL = ("row", "col", "rep")
MESH = pl.DeviceIdType.MESH
GROUPS = 8
AHEAD = 2
LAG = 2


def triangle_kernel(
    outgoing, cols, reps, groups,
    lr_ref, out_ref,
    own, far, outb, inb, hid, got,
    local_sem, in_send, in_recv, ret_local, ret_send, ret_recv, z_send, z_recv,
):
    members = cols * reps
    channels = lr_ref.shape[1]
    per = channels // groups
    width = lr_ref.shape[3]
    height = lr_ref.shape[4]
    row, col, rep = (lax.axis_index(name) for name in ALL)
    me = col * reps + rep
    half = row // 2
    is_mid = (row == 1) | (row == 2)
    mate = half * 4 + 1 - row
    across = 3 - row
    own_index = 0 if outgoing else 1 - half
    far_index = 1 if outgoing else half

    def member(offset):
        return lax.rem(me + offset, members)

    def place(index):
        return (row, index // reps, lax.rem(index, reps))

    barrier = pltpu.get_barrier_semaphore()
    for offset in range(1, members):
        pl.semaphore_signal(barrier, inc=1, device_id=place(member(offset)), device_id_type=MESH)
    pl.semaphore_signal(barrier, inc=1, device_id=(mate, col, rep), device_id_type=MESH)

    @pl.when(is_mid)
    def _():
        pl.semaphore_signal(barrier, inc=1, device_id=(across, col, rep), device_id_type=MESH)

    pl.semaphore_wait(barrier, jnp.where(is_mid, members + 1, members))

    def group(g):
        return pl.ds(g * per, per)

    def strip(index):
        return pl.ds(pl.multiple_of(index * width, width), width)

    def spread(g, offset):
        dest = member(offset)
        return pltpu.make_async_remote_copy(
            src_ref=lr_ref.at[dest, group(g)],
            dst_ref=own.at[group(g), :, strip(me)],
            send_sem=in_send.at[g, offset],
            recv_sem=in_recv.at[g, offset],
            device_id=place(dest),
            device_id_type=MESH,
        )

    def spread_local(g):
        return pltpu.make_async_copy(
            lr_ref.at[me, group(g)], own.at[group(g), :, strip(me)], local_sem.at[g]
        )

    def give_back(g, offset, source):
        dest = member(offset)
        return pltpu.make_async_remote_copy(
            src_ref=source.at[group(g), strip(dest)],
            dst_ref=out_ref.at[pl.ds(me * channels + g * per, per)],
            send_sem=ret_send.at[g, offset],
            recv_sem=ret_recv.at[g, offset],
            device_id=place(dest),
            device_id_type=MESH,
        )

    def give_back_local(g, source):
        return pltpu.make_async_copy(
            source.at[group(g), strip(me)],
            out_ref.at[pl.ds(me * channels + g * per, per)],
            ret_local.at[g],
        )

    def along(g, kind, source, target, to):
        return pltpu.make_async_remote_copy(
            src_ref=source,
            dst_ref=target,
            send_sem=z_send.at[kind, g],
            recv_sem=z_recv.at[kind, g],
            device_id=(to, col, rep),
            device_id_type=MESH,
        )

    def to_middle(g):
        return along(g, 0, own.at[group(g)], far.at[group(g)], mate)

    def across_first(g):
        if outgoing:
            return along(g, 1, own.at[group(g), 1], inb.at[0, group(g)], across)
        return along(g, 1, outb.at[group(g)], inb.at[group(g)], across)

    def across_second(g):
        return along(g, 2, far.at[group(g), 1], inb.at[1, group(g)], across)

    def to_end(g):
        return along(g, 3, hid.at[far_index, group(g)], got.at[group(g)], mate)

    def start_spread(g):
        spread_local(g).start()
        for offset in range(1, members):
            spread(g, offset).start()

    def wait_spread(g):
        spread_local(g).wait()
        for offset in range(1, members):
            spread(g, offset).wait_recv()

    def start_back(g, source):
        give_back_local(g, source).start()
        for offset in range(1, members):
            give_back(g, offset, source).start()

    def finish_back(g, source):
        give_back_local(g, source).wait()
        for offset in range(1, members):
            give_back(g, offset, source).wait()
            spread(g, offset).wait_send()

    for g in range(min(AHEAD, groups)):
        start_spread(g)

    def joined(c, side, rows):
        return jnp.concatenate([own[c, side, rows], far[c, side, rows]], axis=1)

    everything = pl.ds(0, members * width)

    def partial(c, which):
        rows = pl.ds(pl.multiple_of(which * 2 * height, 2 * height), 2 * height)
        return lax.dot_general(
            joined(c, 1, everything),
            joined(c, 0, rows),
            (((1,), (1,)), ((), ())),
            preferred_element_type=jnp.float32,
        )

    def forward(c):
        outb[c] = partial(c, 1 - half).astype(outb.dtype)

    def multiply(c):
        if outgoing:
            left = joined(c, 0, everything)
            blocks = (
                (row, own.at[c, 1]),
                (mate, far.at[c, 1]),
                (across, inb.at[0, c]),
                (3 - mate, inb.at[1, c]),
            )
            for block, right in blocks:
                result = lax.dot_general(
                    right[...],
                    left,
                    (((0,), (0,)), ((), ())),
                    preferred_element_type=jnp.float32,
                ).astype(hid.dtype)
                rows = pl.ds(pl.multiple_of(block * height, height), height)
                hid[0, c, rows] = result[:, :height]
                hid[1, c, rows] = result[:, height:]
        else:
            result = (partial(c, half) + inb[c].astype(jnp.float32)).astype(hid.dtype)
            hid[0, c] = result[:, :height]
            hid[1, c] = result[:, height:]

    def each(g, func):
        lax.fori_loop(0, per, lambda n, _: (func(g * per + n), _)[1], 0)

    @pl.when(is_mid)
    def _():
        back = hid.at[own_index]

        def step(m, carry):
            @pl.when(m + AHEAD < groups)
            def _():
                start_spread(m + AHEAD)

            @pl.when(m < groups)
            def _():
                wait_spread(m)
                if outgoing:
                    across_first(m).start()

            @pl.when((m >= 1) & (m <= groups))
            def _():
                g = m - 1
                to_middle(g).wait_recv()
                if outgoing:
                    across_second(g).start()
                else:
                    each(g, forward)
                    across_first(g).start()

            @pl.when(m >= 2)
            def _():
                g = m - 2
                across_first(g).wait_recv()
                if outgoing:
                    across_second(g).wait_recv()
                each(g, multiply)
                to_end(g).start()
                start_back(g, back)

            return carry

        lax.fori_loop(0, groups + 2, step, 0)

        def drain(g, carry):
            finish_back(g, back)
            across_first(g).wait_send()
            if outgoing:
                across_second(g).wait_send()
            to_end(g).wait_send()
            return carry

        lax.fori_loop(0, groups, drain, 0)

    @pl.when(jnp.logical_not(is_mid))
    def _():
        def step(m, carry):
            @pl.when(m + AHEAD < groups)
            def _():
                start_spread(m + AHEAD)

            @pl.when(m < groups)
            def _():
                wait_spread(m)
                to_middle(m).start()

            @pl.when(m >= LAG)
            def _():
                to_end(m - LAG).wait_recv()
                start_back(m - LAG, got)

            return carry

        lax.fori_loop(0, groups + LAG, step, 0)

        def drain(g, carry):
            finish_back(g, got)
            to_middle(g).wait_send()
            return carry

        lax.fori_loop(0, groups, drain, 0)


def triangle_line(lr, outgoing):
    cols, reps = lax.axis_size("col"), lax.axis_size("rep")
    members, channels, _, width, height = lr.shape
    groups = min(GROUPS, channels)
    long, npair = members * width, 4 * height
    bf16 = jnp.bfloat16
    dma = pltpu.SemaphoreType.DMA
    return pl.pallas_call(
        functools.partial(triangle_kernel, outgoing, cols, reps, groups),
        out_shape=jax.ShapeDtypeStruct((members * channels, width, height), bf16),
        in_specs=[pl.BlockSpec(memory_space=pltpu.VMEM)],
        out_specs=pl.BlockSpec(memory_space=pltpu.VMEM),
        scratch_shapes=[
            pltpu.VMEM((channels, 2, long, height), bf16),
            pltpu.VMEM((channels, 2, long, height), bf16),
            pltpu.VMEM((16, 128) if outgoing else (channels, long, 2 * height), bf16),
            pltpu.VMEM(
                (2, channels, long, height) if outgoing else (channels, long, 2 * height), bf16
            ),
            pltpu.VMEM((2, channels, npair, height), bf16),
            pltpu.VMEM((channels, npair, height), bf16),
            dma((groups,)),
            dma((groups, members)),
            dma((groups, members)),
            dma((groups,)),
            dma((groups, members)),
            dma((groups, members)),
            dma((4, groups)),
            dma((4, groups)),
        ],
        compiler_params=pltpu.CompilerParams(
            collective_id=1 if outgoing else 2,
            has_side_effects=True,
            vmem_limit_bytes=48 * 2**20,
        ),
        cost_estimate=pl.CostEstimate(
            flops=4 * channels * npair * npair * height,
            bytes_accessed=6 * lr.size,
            transcendentals=0,
        ),
        name="triangle_out" if outgoing else "triangle_in",
    )(lr)


def exchange(values, axes):
    return lax.all_to_all(values, axes, split_axis=0, concat_axis=0, tiled=True)


def triangle_any(lr, outgoing):
    rows = lax.axis_size("row")
    members, channels, _, width, height = lr.shape
    per = channels // rows
    grid = lr.reshape(members, rows, per, 2, width, height)
    got = exchange(jnp.moveaxis(grid, 1, 0).reshape(rows * members, per, 2, width, height), ALL)
    grid = got.reshape(rows, members, per, 2, width, height)
    full = jnp.transpose(grid, (3, 2, 1, 4, 0, 5)).reshape(
        2, per, members * width, rows * height
    )
    form = "cka,ckb->cba" if outgoing else "cak,cbk->cba"
    products = jnp.einsum(form, full[0], full[1], preferred_element_type=jnp.float32)
    grid = products.astype(jnp.bfloat16).reshape(per, members, width, rows, height)
    outbound = jnp.transpose(grid, (3, 1, 0, 2, 4)).reshape(-1, per, width, height)
    back = exchange(outbound, ALL).reshape(rows, members, per, width, height)
    return jnp.moveaxis(back, 0, 1).reshape(members * channels, width, height)


def triangle(lr, outgoing):
    if lax.axis_size("row") == 4 and lr.shape[1] % min(GROUPS, lr.shape[1]) == 0:
        return triangle_line(lr, outgoing)
    return triangle_any(lr, outgoing)


def normalize(values, axis):
    mean_value = jnp.mean(values, axis, keepdims=True)
    square_mean = jnp.mean(values * values, axis, keepdims=True)
    return (values - mean_value) * lax.rsqrt(square_mean - mean_value * mean_value + epsilon)


def gated(normed, w_value, w_gate):
    value = jnp.einsum("abd,dc->cab", normed, w_value, preferred_element_type=jnp.float32)
    gate = jnp.einsum("abd,dc->cab", normed, w_gate, preferred_element_type=jnp.float32)
    return (jax.nn.sigmoid(gate) * value).astype(jnp.bfloat16)


def finish(state, normed, returned, w_gate, w_out):
    scaled = normalize(returned.astype(jnp.float32), 0).astype(jnp.bfloat16)
    projected = jnp.einsum("cji,cd->jid", scaled, w_out, preferred_element_type=jnp.float32)
    gate = jax.nn.sigmoid(
        jnp.einsum("jid,de->jie", normed, w_gate, preferred_element_type=jnp.float32)
    )
    return state + gate * projected


def spread_tile(normed, w_left, w_left_gate, w_right, w_right_gate):
    members = lax.axis_size("col") * lax.axis_size("rep")
    pairs = jnp.stack(
        [gated(normed, w_left, w_left_gate), gated(normed, w_right, w_right_gate)], axis=1
    )
    return pairs.reshape(members, -1, *pairs.shape[1:])


def on_device(
    pair, w_left, w_left_gate, w_right, w_right_gate, w_gate, w_out, w_trans_in, w_trans_out
):
    reps = lax.axis_size("rep")
    width = pair.shape[1] // reps
    out_all = lax.all_gather(w_out, "rep", axis=1, tiled=True)
    sides = lax.all_gather(
        jnp.stack([w_left, w_left_gate, w_right, w_right_gate]), "rep", axis=3, tiled=True
    )
    half = lax.dynamic_slice_in_dim(pair, lax.axis_index("rep") * width, width, 1)
    state = jnp.transpose(half, (1, 0, 2)).astype(jnp.float32)
    for index, outgoing in ((0, True), (1, False)):
        normed = normalize(state, 2).astype(jnp.bfloat16)
        lr = spread_tile(normed, *(sides[n, index] for n in range(4)))
        returned = triangle(lr, outgoing)
        state = finish(state, normed, returned, w_gate[index], out_all[index])

    normed = normalize(state, 2).astype(jnp.bfloat16)
    hidden = w_trans_out.shape[0]
    inner = jnp.einsum("jid,de->jie", normed, w_trans_in, preferred_element_type=jnp.float32)
    active = (jax.nn.silu(inner[..., :hidden]) * inner[..., hidden:]).astype(jnp.bfloat16)
    updated = state + jnp.einsum(
        "jie,ed->jid", active, w_trans_out, preferred_element_type=jnp.float32
    )
    return jnp.transpose(updated.astype(jnp.bfloat16), (1, 0, 2))


def solution(mesh):
    placed = (
        P("row", "col", None),
        P(None, None, "rep"),
        P(None, None, "rep"),
        P(None, None, "rep"),
        P(None, None, "rep"),
        P(),
        P(None, "rep", None),
        P(),
        P(),
    )
    return jax.shard_map(
        on_device,
        mesh=mesh,
        in_specs=placed,
        out_specs=P("row", ("col", "rep"), None),
        check_vma=False,
    )
```

```python
import functools

import jax
import jax.numpy as jnp
from jax import lax
from jax.experimental import pallas as pl
from jax.experimental.pallas import tpu as pltpu
from jax.sharding import PartitionSpec as P

epsilon = 1e-05
ALL = ("row", "col", "rep")
MESH = pl.DeviceIdType.MESH
GROUPS = 8
LAG = 3


def triangle_kernel(
    outgoing, cols, reps, groups,
    lr_ref, out_ref,
    own, far, outb, inb, hid, got,
    local_sem, in_send, in_recv, ret_local, ret_send, ret_recv, z_send, z_recv,
):
    members = cols * reps
    channels = lr_ref.shape[1]
    per = channels // groups
    width = lr_ref.shape[3]
    height = lr_ref.shape[4]
    row, col, rep = (lax.axis_index(name) for name in ALL)
    me = col * reps + rep
    half = row // 2
    is_mid = (row == 1) | (row == 2)
    mate = half * 4 + 1 - row
    across = 3 - row
    own_index = 0 if outgoing else 1 - half
    far_index = 1 if outgoing else half

    def member(offset):
        return lax.rem(me + offset, members)

    def place(index):
        return (row, index // reps, lax.rem(index, reps))

    barrier = pltpu.get_barrier_semaphore()
    for offset in range(1, members):
        pl.semaphore_signal(barrier, inc=1, device_id=place(member(offset)), device_id_type=MESH)
    pl.semaphore_signal(barrier, inc=1, device_id=(mate, col, rep), device_id_type=MESH)

    @pl.when(is_mid)
    def _():
        pl.semaphore_signal(barrier, inc=1, device_id=(across, col, rep), device_id_type=MESH)

    pl.semaphore_wait(barrier, jnp.where(is_mid, members + 1, members))

    def group(g):
        return pl.ds(g * per, per)

    def strip(index):
        return pl.ds(pl.multiple_of(index * width, width), width)

    def spread(g, offset):
        dest = member(offset)
        return pltpu.make_async_remote_copy(
            src_ref=lr_ref.at[dest, group(g)],
            dst_ref=own.at[group(g), :, strip(me)],
            send_sem=in_send.at[g, offset],
            recv_sem=in_recv.at[g, offset],
            device_id=place(dest),
            device_id_type=MESH,
        )

    def spread_local(g):
        return pltpu.make_async_copy(
            lr_ref.at[me, group(g)], own.at[group(g), :, strip(me)], local_sem.at[g]
        )

    def give_back(g, offset, source):
        dest = member(offset)
        return pltpu.make_async_remote_copy(
            src_ref=source.at[group(g), strip(dest)],
            dst_ref=out_ref.at[pl.ds(me * channels + g * per, per)],
            send_sem=ret_send.at[g, offset],
            recv_sem=ret_recv.at[g, offset],
            device_id=place(dest),
            device_id_type=MESH,
        )

    def give_back_local(g, source):
        return pltpu.make_async_copy(
            source.at[group(g), strip(me)],
            out_ref.at[pl.ds(me * channels + g * per, per)],
            ret_local.at[g],
        )

    def along(g, kind, source, target, to):
        return pltpu.make_async_remote_copy(
            src_ref=source,
            dst_ref=target,
            send_sem=z_send.at[kind, g],
            recv_sem=z_recv.at[kind, g],
            device_id=(to, col, rep),
            device_id_type=MESH,
        )

    def to_middle(g):
        if outgoing:
            return along(g, 0, own.at[group(g), 1], far.at[group(g), 1], mate)
        return along(g, 0, own.at[group(g)], far.at[group(g)], mate)

    def to_middle_left(g):
        return along(g, 4, own.at[group(g), 0], far.at[group(g), 0], mate)

    def across_first(g):
        if outgoing:
            return along(g, 1, own.at[group(g), 1], inb.at[0, group(g)], across)
        return along(g, 1, outb.at[group(g)], inb.at[group(g)], across)

    def across_second(g):
        return along(g, 2, far.at[group(g), 1], inb.at[1, group(g)], across)

    def to_end(g):
        return along(g, 3, hid.at[far_index, group(g)], got.at[group(g)], mate)

    def start_spread(g):
        spread_local(g).start()
        for offset in range(1, members):
            spread(g, offset).start()

    def wait_spread(g):
        spread_local(g).wait()
        for offset in range(1, members):
            spread(g, offset).wait_recv()

    def start_back(g, source):
        give_back_local(g, source).start()
        for offset in range(1, members):
            give_back(g, offset, source).start()

    def finish_back(g, source):
        give_back_local(g, source).wait()
        for offset in range(1, members):
            give_back(g, offset, source).wait()
            spread(g, offset).wait_send()

    start_spread(0)

    def joined(c, side, rows):
        return jnp.concatenate([own[c, side, rows], far[c, side, rows]], axis=1)

    everything = pl.ds(0, members * width)

    def partial(c, which):
        rows = pl.ds(pl.multiple_of(which * 2 * height, 2 * height), 2 * height)
        return lax.dot_general(
            joined(c, 1, everything),
            joined(c, 0, rows),
            (((1,), (1,)), ((), ())),
            preferred_element_type=jnp.float32,
        )

    def forward(c):
        outb[c] = partial(c, 1 - half).astype(outb.dtype)

    def multiply(c):
        if outgoing:
            left = joined(c, 0, everything)
            blocks = (
                (row, own.at[c, 1]),
                (mate, far.at[c, 1]),
                (across, inb.at[0, c]),
                (3 - mate, inb.at[1, c]),
            )
            for block, right in blocks:
                result = lax.dot_general(
                    right[...],
                    left,
                    (((0,), (0,)), ((), ())),
                    preferred_element_type=jnp.float32,
                ).astype(hid.dtype)
                rows = pl.ds(pl.multiple_of(block * height, height), height)
                hid[0, c, rows] = result[:, :height]
                hid[1, c, rows] = result[:, height:]
        else:
            result = (partial(c, half) + inb[c].astype(jnp.float32)).astype(hid.dtype)
            hid[0, c] = result[:, :height]
            hid[1, c] = result[:, height:]

    def each(g, func):
        lax.fori_loop(0, per, lambda n, _: (func(g * per + n), _)[1], 0)

    @pl.when(is_mid)
    def _():
        back = hid.at[own_index]

        def step(m, carry):
            @pl.when(m < groups)
            def _():
                wait_spread(m)
                if outgoing:
                    across_first(m).start()

            @pl.when(m + 1 < groups)
            def _():
                start_spread(m + 1)

            @pl.when((m >= 1) & (m <= groups))
            def _():
                g = m - 1
                to_middle(g).wait_recv()
                if outgoing:
                    across_second(g).start()
                else:
                    each(g, forward)
                    across_first(g).start()

            @pl.when(m >= 2)
            def _():
                g = m - 2
                across_first(g).wait_recv()
                if outgoing:
                    to_middle_left(g).wait_recv()
                    across_second(g).wait_recv()
                each(g, multiply)
                to_end(g).start()
                start_back(g, back)

            return carry

        lax.fori_loop(0, groups + 2, step, 0)

        def drain(g, carry):
            finish_back(g, back)
            across_first(g).wait_send()
            if outgoing:
                across_second(g).wait_send()
            to_end(g).wait_send()
            return carry

        lax.fori_loop(0, groups, drain, 0)

    @pl.when(jnp.logical_not(is_mid))
    def _():
        def step(m, carry):
            @pl.when(m < groups)
            def _():
                wait_spread(m)
                to_middle(m).start()
                if outgoing:
                    to_middle_left(m).start()

            @pl.when(m + 1 < groups)
            def _():
                start_spread(m + 1)

            @pl.when(m >= LAG)
            def _():
                to_end(m - LAG).wait_recv()
                start_back(m - LAG, got)

            return carry

        lax.fori_loop(0, groups + LAG, step, 0)

        def drain(g, carry):
            finish_back(g, got)
            to_middle(g).wait_send()
            if outgoing:
                to_middle_left(g).wait_send()
            return carry

        lax.fori_loop(0, groups, drain, 0)


def triangle_line(lr, outgoing):
    cols, reps = lax.axis_size("col"), lax.axis_size("rep")
    members, channels, _, width, height = lr.shape
    groups = min(GROUPS, channels)
    long, npair = members * width, 4 * height
    bf16 = jnp.bfloat16
    dma = pltpu.SemaphoreType.DMA
    return pl.pallas_call(
        functools.partial(triangle_kernel, outgoing, cols, reps, groups),
        out_shape=jax.ShapeDtypeStruct((members * channels, width, height), bf16),
        in_specs=[pl.BlockSpec(memory_space=pltpu.VMEM)],
        out_specs=pl.BlockSpec(memory_space=pltpu.VMEM),
        scratch_shapes=[
            pltpu.VMEM((channels, 2, long, height), bf16),
            pltpu.VMEM((channels, 2, long, height), bf16),
            pltpu.VMEM((16, 128) if outgoing else (channels, long, 2 * height), bf16),
            pltpu.VMEM(
                (2, channels, long, height) if outgoing else (channels, long, 2 * height), bf16
            ),
            pltpu.VMEM((2, channels, npair, height), bf16),
            pltpu.VMEM((channels, npair, height), bf16),
            dma((groups,)),
            dma((groups, members)),
            dma((groups, members)),
            dma((groups,)),
            dma((groups, members)),
            dma((groups, members)),
            dma((5, groups)),
            dma((5, groups)),
        ],
        compiler_params=pltpu.CompilerParams(
            collective_id=1 if outgoing else 2,
            has_side_effects=True,
            vmem_limit_bytes=48 * 2**20,
        ),
        cost_estimate=pl.CostEstimate(
            flops=4 * channels * npair * npair * height,
            bytes_accessed=6 * lr.size,
            transcendentals=0,
        ),
        name="triangle_out" if outgoing else "triangle_in",
    )(lr)


def exchange(values, axes):
    return lax.all_to_all(values, axes, split_axis=0, concat_axis=0, tiled=True)


def triangle_any(lr, outgoing):
    rows = lax.axis_size("row")
    members, channels, _, width, height = lr.shape
    per = channels // rows
    grid = lr.reshape(members, rows, per, 2, width, height)
    got = exchange(jnp.moveaxis(grid, 1, 0).reshape(rows * members, per, 2, width, height), ALL)
    grid = got.reshape(rows, members, per, 2, width, height)
    full = jnp.transpose(grid, (3, 2, 1, 4, 0, 5)).reshape(
        2, per, members * width, rows * height
    )
    form = "cka,ckb->cba" if outgoing else "cak,cbk->cba"
    products = jnp.einsum(form, full[0], full[1], preferred_element_type=jnp.float32)
    grid = products.astype(jnp.bfloat16).reshape(per, members, width, rows, height)
    outbound = jnp.transpose(grid, (3, 1, 0, 2, 4)).reshape(-1, per, width, height)
    back = exchange(outbound, ALL).reshape(rows, members, per, width, height)
    return jnp.moveaxis(back, 0, 1).reshape(members * channels, width, height)


def triangle(lr, outgoing):
    if lax.axis_size("row") == 4 and lr.shape[1] % min(GROUPS, lr.shape[1]) == 0:
        return triangle_line(lr, outgoing)
    return triangle_any(lr, outgoing)


def normalize(values, axis):
    mean_value = jnp.mean(values, axis, keepdims=True)
    square_mean = jnp.mean(values * values, axis, keepdims=True)
    return (values - mean_value) * lax.rsqrt(square_mean - mean_value * mean_value + epsilon)


def finish(state, normed, returned, w_gate, w_out):
    scaled = normalize(returned.astype(jnp.float32), 0).astype(jnp.bfloat16)
    projected = jnp.einsum("cji,cd->jid", scaled, w_out, preferred_element_type=jnp.float32)
    gate = jax.nn.sigmoid(
        jnp.einsum("jid,de->jie", normed, w_gate, preferred_element_type=jnp.float32)
    )
    return state + gate * projected


def squash(values):
    return 0.5 * jnp.tanh(0.5 * values) + 0.5


def project_kernel(state_ref, weight_ref, normed_ref, lr_ref, turned):
    channels = lr_ref.shape[0]
    normed = normalize(state_ref[...], 2).astype(jnp.bfloat16)
    normed_ref[...] = normed
    for n in range(normed.shape[0]):
        linear = lax.dot_general(
            weight_ref[...],
            normed[n],
            (((1,), (1,)), ((), ())),
            preferred_element_type=jnp.float32,
        )
        for side in range(2):
            first = 2 * side * channels
            value = linear[first : first + channels]
            gate = linear[first + channels : first + 2 * channels]
            turned[:, side, n, :] = squash(gate) * value
    lr_ref[...] = turned[...].astype(lr_ref.dtype)


def project(state, weight):
    width, height, depth = state.shape
    channels = weight.shape[0] // 4
    block = 8
    return pl.pallas_call(
        project_kernel,
        grid=(width // block,),
        out_shape=(
            jax.ShapeDtypeStruct(state.shape, jnp.bfloat16),
            jax.ShapeDtypeStruct((channels, 2, width, height), jnp.bfloat16),
        ),
        in_specs=[
            pl.BlockSpec((block, height, depth), lambda n: (n, 0, 0)),
            pl.BlockSpec(weight.shape, lambda n: (0, 0)),
        ],
        out_specs=(
            pl.BlockSpec((block, height, depth), lambda n: (n, 0, 0)),
            pl.BlockSpec((channels, 2, block, height), lambda n: (0, 0, n, 0)),
        ),
        scratch_shapes=[pltpu.VMEM((channels, 2, block, height), jnp.float32)],
        compiler_params=pltpu.CompilerParams(vmem_limit_bytes=40 * 2**20),
        cost_estimate=pl.CostEstimate(
            flops=2 * state.size * weight.shape[0],
            bytes_accessed=10 * state.size,
            transcendentals=2 * state.size,
        ),
        name="project",
    )(state, weight)


def transition_kernel(state_ref, w_in_ref, w_out_ref, out_ref, turned):
    block, height, depth = state_ref.shape
    hidden = w_out_ref.shape[0]
    state = state_ref[...].reshape(block * height, depth)
    normed = normalize(state, 1).astype(jnp.bfloat16)
    inner = jnp.dot(normed, w_in_ref[...], preferred_element_type=jnp.float32)
    gate = inner[:, :hidden]
    active = gate * squash(gate) * inner[:, hidden:]
    updated = state + jnp.dot(
        active.astype(jnp.bfloat16), w_out_ref[...], preferred_element_type=jnp.float32
    )
    for n in range(block):
        turned[:, n, :] = updated[n * height : (n + 1) * height]
    out_ref[...] = turned[...].astype(out_ref.dtype)


def transition(state, w_trans_in, w_trans_out):
    width, height, depth = state.shape
    block = 8
    return pl.pallas_call(
        transition_kernel,
        grid=(width // block,),
        out_shape=jax.ShapeDtypeStruct((height, width, depth), jnp.bfloat16),
        in_specs=[
            pl.BlockSpec((block, height, depth), lambda n: (n, 0, 0)),
            pl.BlockSpec(w_trans_in.shape, lambda n: (0, 0)),
            pl.BlockSpec(w_trans_out.shape, lambda n: (0, 0)),
        ],
        out_specs=pl.BlockSpec((height, block, depth), lambda n: (0, n, 0)),
        scratch_shapes=[pltpu.VMEM((height, block, depth), jnp.float32)],
        compiler_params=pltpu.CompilerParams(vmem_limit_bytes=40 * 2**20),
        cost_estimate=pl.CostEstimate(
            flops=6 * state.size * w_trans_out.shape[0],
            bytes_accessed=6 * state.size,
            transcendentals=state.size * w_trans_out.shape[0] // depth,
        ),
        name="transition",
    )(state, w_trans_in, w_trans_out)


def on_device(
    pair, w_left, w_left_gate, w_right, w_right_gate, w_gate, w_out, w_trans_in, w_trans_out
):
    reps = lax.axis_size("rep")
    width = pair.shape[1] // reps
    out_all = lax.all_gather(w_out, "rep", axis=1, tiled=True)
    sides = lax.all_gather(
        jnp.stack([w_left, w_left_gate, w_right, w_right_gate]), "rep", axis=3, tiled=True
    )
    half = lax.dynamic_slice_in_dim(pair, lax.axis_index("rep") * width, width, 1)
    state = jnp.transpose(half, (1, 0, 2)).astype(jnp.float32)
    members = lax.axis_size("col") * reps
    weights = jnp.transpose(sides, (1, 0, 3, 2)).reshape(2, -1, sides.shape[2])
    for index, outgoing in ((0, True), (1, False)):
        normed, lr = project(state, weights[index])
        returned = triangle(lr.reshape(members, -1, *lr.shape[1:]), outgoing)
        state = finish(state, normed, returned, w_gate[index], out_all[index])
    return transition(state, w_trans_in, w_trans_out)


def solution(mesh):
    placed = (
        P("row", "col", None),
        P(None, None, "rep"),
        P(None, None, "rep"),
        P(None, None, "rep"),
        P(None, None, "rep"),
        P(),
        P(None, "rep", None),
        P(),
        P(),
    )
    return jax.shard_map(
        on_device,
        mesh=mesh,
        in_specs=placed,
        out_specs=P("row", ("col", "rep"), None),
        check_vma=False,
    )
```

```python
import functools

import jax
import jax.numpy as jnp
from jax import lax
from jax.experimental import pallas as pl
from jax.experimental.pallas import tpu as pltpu
from jax.sharding import PartitionSpec as P

epsilon = 1e-05
ALL = ("row", "col", "rep")
MESH = pl.DeviceIdType.MESH
GROUPS = 8
LAG = 3


def triangle_kernel(
    outgoing, cols, reps, groups,
    lr_ref, out_ref,
    own, far, outb, inb, hid, got,
    local_sem, in_send, in_recv, ret_local, ret_send, ret_recv, z_send, z_recv,
):
    members = cols * reps
    channels = lr_ref.shape[1]
    per = channels // groups
    width = lr_ref.shape[3]
    height = lr_ref.shape[4]
    row, col, rep = (lax.axis_index(name) for name in ALL)
    me = col * reps + rep
    half = row // 2
    is_mid = (row == 1) | (row == 2)
    mate = half * 4 + 1 - row
    across = 3 - row
    own_index = 0 if outgoing else 1 - half
    far_index = 1 if outgoing else half

    def member(offset):
        return lax.rem(me + offset, members)

    def place(index):
        return (row, index // reps, lax.rem(index, reps))

    barrier = pltpu.get_barrier_semaphore()
    for offset in range(1, members):
        pl.semaphore_signal(barrier, inc=1, device_id=place(member(offset)), device_id_type=MESH)
    pl.semaphore_signal(barrier, inc=1, device_id=(mate, col, rep), device_id_type=MESH)

    @pl.when(is_mid)
    def _():
        pl.semaphore_signal(barrier, inc=1, device_id=(across, col, rep), device_id_type=MESH)

    pl.semaphore_wait(barrier, jnp.where(is_mid, members + 1, members))

    def group(g):
        return pl.ds(g * per, per)

    def strip(index):
        return pl.ds(pl.multiple_of(index * width, width), width)

    def spread(g, offset):
        dest = member(offset)
        return pltpu.make_async_remote_copy(
            src_ref=lr_ref.at[dest, group(g)],
            dst_ref=own.at[group(g), :, strip(me)],
            send_sem=in_send.at[g, offset],
            recv_sem=in_recv.at[g, offset],
            device_id=place(dest),
            device_id_type=MESH,
        )

    def spread_local(g):
        return pltpu.make_async_copy(
            lr_ref.at[me, group(g)], own.at[group(g), :, strip(me)], local_sem.at[g]
        )

    def give_back(g, offset, source):
        dest = member(offset)
        return pltpu.make_async_remote_copy(
            src_ref=source.at[group(g), strip(dest)],
            dst_ref=out_ref.at[pl.ds(me * channels + g * per, per)],
            send_sem=ret_send.at[g, offset],
            recv_sem=ret_recv.at[g, offset],
            device_id=place(dest),
            device_id_type=MESH,
        )

    def give_back_local(g, source):
        return pltpu.make_async_copy(
            source.at[group(g), strip(me)],
            out_ref.at[pl.ds(me * channels + g * per, per)],
            ret_local.at[g],
        )

    def along(c, kind, source, target, to):
        return pltpu.make_async_remote_copy(
            src_ref=source,
            dst_ref=target,
            send_sem=z_send.at[kind, c],
            recv_sem=z_recv.at[kind, c],
            device_id=(to, col, rep),
            device_id_type=MESH,
        )

    def to_middle(c):
        if outgoing:
            return along(c, 0, own.at[c, 1], far.at[c, 1], mate)
        return along(c, 0, own.at[c], far.at[c], mate)

    def to_middle_left(c):
        return along(c, 4, own.at[c, 0], far.at[c, 0], mate)

    def across_first(c):
        if outgoing:
            return along(c, 1, own.at[c, 1], inb.at[0, c], across)
        return along(c, 1, outb.at[c], inb.at[c], across)

    def across_second(c):
        return along(c, 2, far.at[c, 1], inb.at[1, c], across)

    def to_end(c):
        return along(c, 3, hid.at[far_index, c], got.at[c], mate)

    def start_spread(g):
        spread_local(g).start()
        for offset in range(1, members):
            spread(g, offset).start()

    def wait_spread(g):
        spread_local(g).wait()
        for offset in range(1, members):
            spread(g, offset).wait_recv()

    def start_back(g, source):
        give_back_local(g, source).start()
        for offset in range(1, members):
            give_back(g, offset, source).start()

    def finish_back(g, source):
        give_back_local(g, source).wait()
        for offset in range(1, members):
            give_back(g, offset, source).wait()
            spread(g, offset).wait_send()

    start_spread(0)

    def joined(c, side, rows):
        return jnp.concatenate([own[c, side, rows], far[c, side, rows]], axis=1)

    everything = pl.ds(0, members * width)

    def partial(c, which):
        rows = pl.ds(pl.multiple_of(which * 2 * height, 2 * height), 2 * height)
        return lax.dot_general(
            joined(c, 1, everything),
            joined(c, 0, rows),
            (((1,), (1,)), ((), ())),
            preferred_element_type=jnp.float32,
        )

    def forward(c):
        outb[c] = partial(c, 1 - half).astype(outb.dtype)

    def multiply(c):
        if outgoing:
            left = joined(c, 0, everything)
            blocks = (
                (row, own.at[c, 1]),
                (mate, far.at[c, 1]),
                (across, inb.at[0, c]),
                (3 - mate, inb.at[1, c]),
            )
            for block, right in blocks:
                result = lax.dot_general(
                    right[...],
                    left,
                    (((0,), (0,)), ((), ())),
                    preferred_element_type=jnp.float32,
                ).astype(hid.dtype)
                rows = pl.ds(pl.multiple_of(block * height, height), height)
                hid[0, c, rows] = result[:, :height]
                hid[1, c, rows] = result[:, height:]
        else:
            result = (partial(c, half) + inb[c].astype(jnp.float32)).astype(hid.dtype)
            hid[0, c] = result[:, :height]
            hid[1, c] = result[:, height:]

    def each(g, func):
        lax.fori_loop(0, per, lambda n, _: (func(g * per + n), _)[1], 0)

    def offer(c):
        across_first(c).start()

    def pass_on(c):
        to_middle(c).wait_recv()
        if outgoing:
            across_second(c).start()
        else:
            forward(c)
            across_first(c).start()

    def complete(c):
        across_first(c).wait_recv()
        if outgoing:
            to_middle_left(c).wait_recv()
            across_second(c).wait_recv()
        multiply(c)
        to_end(c).start()

    def hand_in(c):
        to_middle(c).start()
        if outgoing:
            to_middle_left(c).start()

    def middle_sent(c):
        across_first(c).wait_send()
        if outgoing:
            across_second(c).wait_send()
        to_end(c).wait_send()

    def end_sent(c):
        to_middle(c).wait_send()
        if outgoing:
            to_middle_left(c).wait_send()

    @pl.when(is_mid)
    def _():
        back = hid.at[own_index]

        def step(m, carry):
            @pl.when(m < groups)
            def _():
                wait_spread(m)
                if outgoing:
                    each(m, offer)

            @pl.when(m + 1 < groups)
            def _():
                start_spread(m + 1)

            @pl.when((m >= 1) & (m <= groups))
            def _():
                each(m - 1, pass_on)

            @pl.when(m >= 2)
            def _():
                each(m - 2, complete)
                start_back(m - 2, back)

            return carry

        lax.fori_loop(0, groups + 2, step, 0)

        def drain(g, carry):
            finish_back(g, back)
            each(g, middle_sent)
            return carry

        lax.fori_loop(0, groups, drain, 0)

    @pl.when(jnp.logical_not(is_mid))
    def _():
        def step(m, carry):
            @pl.when(m < groups)
            def _():
                wait_spread(m)
                each(m, hand_in)

            @pl.when(m + 1 < groups)
            def _():
                start_spread(m + 1)

            @pl.when(m >= LAG)
            def _():
                each(m - LAG, lambda c: to_end(c).wait_recv())
                start_back(m - LAG, got)

            return carry

        lax.fori_loop(0, groups + LAG, step, 0)

        def drain(g, carry):
            finish_back(g, got)
            each(g, end_sent)
            return carry

        lax.fori_loop(0, groups, drain, 0)


def triangle_line(lr, outgoing):
    cols, reps = lax.axis_size("col"), lax.axis_size("rep")
    members, channels, _, width, height = lr.shape
    groups = min(GROUPS, channels)
    long, npair = members * width, 4 * height
    bf16 = jnp.bfloat16
    dma = pltpu.SemaphoreType.DMA
    return pl.pallas_call(
        functools.partial(triangle_kernel, outgoing, cols, reps, groups),
        out_shape=jax.ShapeDtypeStruct((members * channels, width, height), bf16),
        in_specs=[pl.BlockSpec(memory_space=pltpu.VMEM)],
        out_specs=pl.BlockSpec(memory_space=pltpu.VMEM),
        scratch_shapes=[
            pltpu.VMEM((channels, 2, long, height), bf16),
            pltpu.VMEM((channels, 2, long, height), bf16),
            pltpu.VMEM((16, 128) if outgoing else (channels, long, 2 * height), bf16),
            pltpu.VMEM(
                (2, channels, long, height) if outgoing else (channels, long, 2 * height), bf16
            ),
            pltpu.VMEM((2, channels, npair, height), bf16),
            pltpu.VMEM((channels, npair, height), bf16),
            dma((groups,)),
            dma((groups, members)),
            dma((groups, members)),
            dma((groups,)),
            dma((groups, members)),
            dma((groups, members)),
            dma((5, channels)),
            dma((5, channels)),
        ],
        compiler_params=pltpu.CompilerParams(
            collective_id=1 if outgoing else 2,
            has_side_effects=True,
            vmem_limit_bytes=48 * 2**20,
        ),
        cost_estimate=pl.CostEstimate(
            flops=4 * channels * npair * npair * height,
            bytes_accessed=6 * lr.size,
            transcendentals=0,
        ),
        name="triangle_out" if outgoing else "triangle_in",
    )(lr)


def exchange(values, axes):
    return lax.all_to_all(values, axes, split_axis=0, concat_axis=0, tiled=True)


def triangle_any(lr, outgoing):
    rows = lax.axis_size("row")
    members, channels, _, width, height = lr.shape
    per = channels // rows
    grid = lr.reshape(members, rows, per, 2, width, height)
    got = exchange(jnp.moveaxis(grid, 1, 0).reshape(rows * members, per, 2, width, height), ALL)
    grid = got.reshape(rows, members, per, 2, width, height)
    full = jnp.transpose(grid, (3, 2, 1, 4, 0, 5)).reshape(
        2, per, members * width, rows * height
    )
    form = "cka,ckb->cba" if outgoing else "cak,cbk->cba"
    products = jnp.einsum(form, full[0], full[1], preferred_element_type=jnp.float32)
    grid = products.astype(jnp.bfloat16).reshape(per, members, width, rows, height)
    outbound = jnp.transpose(grid, (3, 1, 0, 2, 4)).reshape(-1, per, width, height)
    back = exchange(outbound, ALL).reshape(rows, members, per, width, height)
    return jnp.moveaxis(back, 0, 1).reshape(members * channels, width, height)


def triangle(lr, outgoing):
    if lax.axis_size("row") == 4 and lr.shape[1] % min(GROUPS, lr.shape[1]) == 0:
        return triangle_line(lr, outgoing)
    return triangle_any(lr, outgoing)


def normalize(values, axis):
    mean_value = jnp.mean(values, axis, keepdims=True)
    square_mean = jnp.mean(values * values, axis, keepdims=True)
    return (values - mean_value) * lax.rsqrt(square_mean - mean_value * mean_value + epsilon)


def finish(state, normed, returned, w_gate, w_out):
    scaled = normalize(returned.astype(jnp.float32), 0).astype(jnp.bfloat16)
    projected = jnp.einsum("cji,cd->jid", scaled, w_out, preferred_element_type=jnp.float32)
    gate = jax.nn.sigmoid(
        jnp.einsum("jid,de->jie", normed, w_gate, preferred_element_type=jnp.float32)
    )
    return state + gate * projected


def squash(values):
    return 0.5 * jnp.tanh(0.5 * values) + 0.5


def project_kernel(state_ref, weight_ref, normed_ref, lr_ref, turned):
    channels = lr_ref.shape[0]
    normed = normalize(state_ref[...], 2).astype(jnp.bfloat16)
    normed_ref[...] = normed
    for n in range(normed.shape[0]):
        linear = lax.dot_general(
            weight_ref[...],
            normed[n],
            (((1,), (1,)), ((), ())),
            preferred_element_type=jnp.float32,
        )
        for side in range(2):
            first = 2 * side * channels
            value = linear[first : first + channels]
            gate = linear[first + channels : first + 2 * channels]
            turned[:, side, n, :] = squash(gate) * value
    lr_ref[...] = turned[...].astype(lr_ref.dtype)


def project(state, weight):
    width, height, depth = state.shape
    channels = weight.shape[0] // 4
    block = 8
    return pl.pallas_call(
        project_kernel,
        grid=(width // block,),
        out_shape=(
            jax.ShapeDtypeStruct(state.shape, jnp.bfloat16),
            jax.ShapeDtypeStruct((channels, 2, width, height), jnp.bfloat16),
        ),
        in_specs=[
            pl.BlockSpec((block, height, depth), lambda n: (n, 0, 0)),
            pl.BlockSpec(weight.shape, lambda n: (0, 0)),
        ],
        out_specs=(
            pl.BlockSpec((block, height, depth), lambda n: (n, 0, 0)),
            pl.BlockSpec((channels, 2, block, height), lambda n: (0, 0, n, 0)),
        ),
        scratch_shapes=[pltpu.VMEM((channels, 2, block, height), jnp.float32)],
        compiler_params=pltpu.CompilerParams(vmem_limit_bytes=40 * 2**20),
        cost_estimate=pl.CostEstimate(
            flops=2 * state.size * weight.shape[0],
            bytes_accessed=10 * state.size,
            transcendentals=2 * state.size,
        ),
        name="project",
    )(state, weight)


def transition_kernel(state_ref, w_in_ref, w_out_ref, out_ref, turned):
    block, height, depth = state_ref.shape
    hidden = w_out_ref.shape[0]
    state = state_ref[...].reshape(block * height, depth)
    normed = normalize(state, 1).astype(jnp.bfloat16)
    inner = jnp.dot(normed, w_in_ref[...], preferred_element_type=jnp.float32)
    gate = inner[:, :hidden]
    active = gate * squash(gate) * inner[:, hidden:]
    updated = state + jnp.dot(
        active.astype(jnp.bfloat16), w_out_ref[...], preferred_element_type=jnp.float32
    )
    for n in range(block):
        turned[:, n, :] = updated[n * height : (n + 1) * height]
    out_ref[...] = turned[...].astype(out_ref.dtype)


def transition(state, w_trans_in, w_trans_out):
    width, height, depth = state.shape
    block = 8
    return pl.pallas_call(
        transition_kernel,
        grid=(width // block,),
        out_shape=jax.ShapeDtypeStruct((height, width, depth), jnp.bfloat16),
        in_specs=[
            pl.BlockSpec((block, height, depth), lambda n: (n, 0, 0)),
            pl.BlockSpec(w_trans_in.shape, lambda n: (0, 0)),
            pl.BlockSpec(w_trans_out.shape, lambda n: (0, 0)),
        ],
        out_specs=pl.BlockSpec((height, block, depth), lambda n: (0, n, 0)),
        scratch_shapes=[pltpu.VMEM((height, block, depth), jnp.float32)],
        compiler_params=pltpu.CompilerParams(vmem_limit_bytes=40 * 2**20),
        cost_estimate=pl.CostEstimate(
            flops=6 * state.size * w_trans_out.shape[0],
            bytes_accessed=6 * state.size,
            transcendentals=state.size * w_trans_out.shape[0] // depth,
        ),
        name="transition",
    )(state, w_trans_in, w_trans_out)


def on_device(
    pair, w_left, w_left_gate, w_right, w_right_gate, w_gate, w_out, w_trans_in, w_trans_out
):
    reps = lax.axis_size("rep")
    width = pair.shape[1] // reps
    out_all = lax.all_gather(w_out, "rep", axis=1, tiled=True)
    sides = lax.all_gather(
        jnp.stack([w_left, w_left_gate, w_right, w_right_gate]), "rep", axis=3, tiled=True
    )
    half = lax.dynamic_slice_in_dim(pair, lax.axis_index("rep") * width, width, 1)
    state = jnp.transpose(half, (1, 0, 2)).astype(jnp.float32)
    members = lax.axis_size("col") * reps
    weights = jnp.transpose(sides, (1, 0, 3, 2)).reshape(2, -1, sides.shape[2])
    for index, outgoing in ((0, True), (1, False)):
        normed, lr = project(state, weights[index])
        returned = triangle(lr.reshape(members, -1, *lr.shape[1:]), outgoing)
        state = finish(state, normed, returned, w_gate[index], out_all[index])
    return transition(state, w_trans_in, w_trans_out)


def solution(mesh):
    placed = (
        P("row", "col", None),
        P(None, None, "rep"),
        P(None, None, "rep"),
        P(None, None, "rep"),
        P(None, None, "rep"),
        P(),
        P(None, "rep", None),
        P(),
        P(),
    )
    return jax.shard_map(
        on_device,
        mesh=mesh,
        in_specs=placed,
        out_specs=P("row", ("col", "rep"), None),
        check_vma=False,
    )
```
